512 devices in a mesh: mem: 64 (over y_hi, z, core), gx: 8 (over y_lo, x).
Axes of the slice: x: 4, y: 8 (y_hi: 4, y_lo: 2; y = y_hi * 2 + y_lo), z: 8, core: 2. Of those that a mesh axis runs over, the one named last changes fastest.
Arguments:
- fields: float32 [64, 4, 128, 32, 128], P('mem', None, 'gx'), may hold values from -4 to 9
- precursor: float32 [12, 4096], P(None, 'mem'), may hold values from -5 to 5
- heights: int32 [128, 32], replicated, may hold values from 0 to 32
- param_index: int32 [64, 2], P('mem'), may hold values from 0 to 15
- drag_table: float32 [16], replicated, may hold values from 0.2 to 2
- rough_table: float32 [16], replicated, may hold values from 0.01 to 0.5
Outputs:
- advanced: float32 [64, 4, 128, 32, 128], P('mem', None, 'gx')
The draws below stay inside these ranges and needn't reach their ends.
All inputs are finite; a program needn't handle non-finite values.
Results may differ from the reference program's by a relative error of at most 0.0003.
Values sent between devices are 32-bit elements; how exact they have to be, the bound alone decides.
No kernel may reach another device: no remote copies, remote signals or barrier semaphores. Data moves between devices by JAX's collectives and lax.ppermute only.
A program may use at most 64 MiB of HBM per device.

```python
import math
import jax
import jax.numpy as jnp
from jax import lax

NY = 32
NZ = 128
NPARAM = 16
NX = 128
MEMBERS = 64


def mode_profile(key, amplitude):
    amp_key, wave_key = jax.random.split(key)
    amps = jax.random.uniform(amp_key, (MEMBERS, 3), jnp.float32, -amplitude, amplitude)
    waves = jax.random.uniform(wave_key, (MEMBERS, 3), jnp.float32, 1.0, 5.0)
    position = jnp.arange(NX, dtype=jnp.float32) / NX
    first = amps[:, 0:1] * jnp.sin(3.14159265 * waves[:, 0:1] * position[None, :])
    second = amps[:, 1:2] * jnp.sin(3.14159265 * waves[:, 1:2] * position[None, :])
    third = amps[:, 2:3] * jnp.sin(3.14159265 * waves[:, 2:3] * position[None, :])
    return first + second + third


def draw_fields(key, part):
    key = jax.random.fold_in(key, 11)
    noise_key, mode_key = jax.random.split(key)
    shape = (MEMBERS, 4, NX, NY, NZ)
    position = jnp.arange(NX, dtype=jnp.float32) / NX
    channel = lax.broadcasted_iota(jnp.int32, shape, 1)
    noise = jnp.clip(jax.random.normal(noise_key, shape, jnp.float32), -4.0, 4.0)
    base = 5.0 - 2.5 * position
    bumps = mode_profile(mode_key, 0.6)
    mean_u = (base[None, :] + bumps)[:, None, :, None, None]
    values = jnp.where(channel == 0, mean_u + 0.5 * noise, noise)
    values = jnp.where(channel == 1, 0.5 * noise, values)
    values = jnp.where(channel == 2, 0.3 * noise, values)
    return values.astype(jnp.float32)


def draw_precursor(key, part):
    key = jax.random.fold_in(key, 7)
    rest_key, sign_key, size_key = jax.random.split(key, 3)
    shape = (12, NY * NZ)
    row = lax.broadcasted_iota(jnp.int32, shape, 0)
    rest = jnp.clip(jax.random.normal(rest_key, shape, jnp.float32), -4.0, 4.0)
    signs = jnp.where(jax.random.bernoulli(sign_key, 0.5, shape), 1.0, -1.0)
    far = signs * jax.random.uniform(size_key, shape, jnp.float32, 4.5, 5.0)
    values = jnp.where(row % 3 == 0, far, rest)
    return values.astype(jnp.float32)


def plant(values, key, low, high):
    shape = values.shape
    spot = [jax.random.randint(jax.random.fold_in(key, axis), (), 0, shape[axis]) for axis in range(len(shape))]
    values = values.at[tuple(spot)].set(low)
    longest = shape.index(max(shape))
    spot[longest] = (spot[longest] + 1) % shape[longest]
    return values.at[tuple(spot)].set(high)


def setup_inputs(seed: int = 0) -> dict:
    streams_of = jax.random.split(jax.random.key(seed), 7)
    return {
        "fields": draw_fields(jax.random.fold_in(streams_of[6], 71), 0),
        "precursor": draw_precursor(jax.random.fold_in(streams_of[6], 71), 0),
        "heights": plant(jax.random.randint(streams_of[2], (NX, NY), 0, NZ // 4 + 1), jax.random.fold_in(streams_of[2], 1), 0, (NZ // 4 + 1) - 1).astype(jnp.int32),
        "param_index": plant(jax.random.randint(streams_of[3], (MEMBERS, 2), 0, NPARAM), jax.random.fold_in(streams_of[3], 1), 0, NPARAM - 1).astype(jnp.int32),
        "drag_table": jnp.clip(jnp.exp(jax.random.uniform(streams_of[4], (NPARAM,), jnp.float32, math.log(0.2), math.log(2.0))), 0.2, 2.0),
        "rough_table": jnp.clip(jnp.exp(jax.random.uniform(streams_of[5], (NPARAM,), jnp.float32, math.log(0.01), math.log(0.5))), 0.01, 0.5),
    }


spacing = 2.0
time_step = 0.2
viscosity = 1.0
target_speed = 3.0
relax_time = 1.0
karman = 0.4
buoyancy = 0.0327

def tendency(extended, columns, drag_coef, surface_coef, forcing):
    length = extended.shape[1] - 6

    def shift_x(k):
        return extended[:, 3 + k:3 + k + length]
    center = shift_x(0)

    def shift_y(k):
        return jnp.roll(center, -k, axis=2)
    speed_u = center[0:1]
    speed_v = center[1:2]
    speed_w = center[2:3]
    cen_x = (-shift_x(-3) + 9.0 * shift_x(-2) - 45.0 * shift_x(-1) + 45.0 * shift_x(1) - 9.0 * shift_x(2) + shift_x(3)) / (60.0 * spacing)
    dis_x = (-shift_x(-3) + 6.0 * shift_x(-2) - 15.0 * shift_x(-1) + 20.0 * center - 15.0 * shift_x(1) + 6.0 * shift_x(2) - shift_x(3)) / (60.0 * spacing)
    cen_y = (-shift_y(-3) + 9.0 * shift_y(-2) - 45.0 * shift_y(-1) + 45.0 * shift_y(1) - 9.0 * shift_y(2) + shift_y(3)) / (60.0 * spacing)
    dis_y = (-shift_y(-3) + 6.0 * shift_y(-2) - 15.0 * shift_y(-1) + 20.0 * center - 15.0 * shift_y(1) + 6.0 * shift_y(2) - shift_y(3)) / (60.0 * spacing)
    padded = jnp.pad(center, ((0, 0), (0, 0), (0, 0), (1, 1)))
    above = padded[..., 2:]
    below = padded[..., :-2]
    advection = speed_u * cen_x + jnp.abs(speed_u) * dis_x + speed_v * cen_y + jnp.abs(speed_v) * dis_y + speed_w * (above - below) / (2.0 * spacing)
    laplacian = (shift_x(1) + shift_x(-1) + shift_y(1) + shift_y(-1) + above + below - 6.0 * center) / (spacing * spacing)
    level = lax.broadcasted_iota(jnp.int32, center.shape[1:], 2)
    inside = (level < columns[:, :, None]).astype(jnp.float32)
    lowest = (level == 0).astype(jnp.float32)
    speed = jnp.sqrt(speed_u[0] * speed_u[0] + speed_v[0] * speed_v[0] + speed_w[0] * speed_w[0])
    horizontal = jnp.array([1.0, 1.0, 0.0, 0.0], jnp.float32)[:, None, None, None]
    first_only = jnp.array([1.0, 0.0, 0.0, 0.0], jnp.float32)[:, None, None, None]
    result = -advection + viscosity * laplacian - drag_coef * inside * speed * center
    result = result - surface_coef * speed * lowest * horizontal * center / spacing
    result = result + forcing * first_only
    lifted = buoyancy * center[3]
    result = result.at[2].add(lifted)
    return result

def coefficients(indices, drag_table, rough_table):
    slots = jnp.arange(drag_table.shape[0], dtype=jnp.int32)
    drag_coef = jnp.sum(jnp.where(slots == indices[0], drag_table, 0.0))
    rough = jnp.sum(jnp.where(slots == indices[1], rough_table, 0.0))
    surface_coef = (karman / jnp.log(0.5 * spacing / rough)) ** 2
    return (drag_coef, surface_coef)

def reference(fields, precursor, heights, param_index, drag_table, rough_table):
    plane = precursor.reshape(4, 3, NY, NZ)

    def one_member(items):
        start, indices = items
        drag_coef, surface_coef = coefficients(indices, drag_table, rough_table)
        current = start
        for fraction in (1.0 / 3.0, 0.5):
            forcing = (target_speed - jnp.sum(current[0]) / (NX * NY * NZ)) / relax_time
            outlet = jnp.repeat(current[:, -1:], 3, axis=1)
            extended = jnp.concatenate([plane, current, outlet], axis=1)
            current = start + fraction * time_step * tendency(extended, heights, drag_coef, surface_coef, forcing)
        return current
    return lax.map(one_member, (fields, param_index))
```

```python
import functools

import jax
import jax.numpy as jnp
from jax import lax
from jax.experimental import pallas as pl
from jax.experimental.pallas import tpu as pltpu
from jax.sharding import PartitionSpec as P

spacing = 2.0
time_step = 0.2
viscosity = 1.0
target_speed = 3.0
relax_time = 1.0
karman = 0.4
buoyancy = 0.0327

SUB = 8
FIRST = time_step / 3.0
SECOND = time_step / 2.0


def wrap_rows(ref, field, layer, span):
    ref[field, layer, pl.ds(SUB - 3, 3), :] = ref[field, layer, pl.ds(SUB + span - 3, 3), :]
    ref[field, layer, pl.ds(SUB + span, 3), :] = ref[field, layer, pl.ds(SUB, 3), :]


def direction(speed, scale, diffuse):
    slow = speed * scale
    size = jnp.abs(slow)
    near = 15.0 * size + diffuse
    wide = 45.0 * slow
    odd = 9.0 * slow
    even = 6.0 * size
    return (
        {
            1: near - wide,
            -1: near + wide,
            2: odd - even,
            -2: -(odd + even),
            3: size - slow,
            -3: size + slow,
        },
        20.0 * size,
    )


def stage_chunk(state, layer, chunk, step, drag, surface, levels):
    row = SUB + SUB * chunk

    def load(field, dx, dy):
        return state[field, layer + 3 + dx, pl.ds(row + dy, SUB), :]

    centre = [load(f, 0, 0) for f in range(4)]
    u, v, w = centre[:3]
    diffuse = step * viscosity / (spacing * spacing)
    scale = step / (60.0 * spacing)
    along_x, mid_x = direction(u, scale, diffuse)
    along_y, mid_y = direction(v, scale, diffuse)
    lane = lax.broadcasted_iota(jnp.int32, u.shape, 1)
    lift = w * (step / (2.0 * spacing))
    up = jnp.where(lane == levels - 1, 0.0, diffuse - lift)
    down = jnp.where(lane == 0, 0.0, diffuse + lift)
    speed = jnp.sqrt(u * u + v * v + w * w)
    middle = -(mid_x + mid_y + 6.0 * diffuse + speed * drag)
    middle_uv = middle - jnp.where(lane == 0, speed * surface, 0.0)
    out = []
    for f in range(4):
        s = centre[f]
        total = (middle_uv if f < 2 else middle) * s
        total = total + up * pltpu.roll(s, levels - 1, 1) + down * pltpu.roll(s, 1, 1)
        for k in (1, -1, 2, -2, 3, -3):
            total = total + along_x[k] * load(f, k, 0)
            total = total + along_y[k] * load(f, 0, k)
        if f == 2:
            total = total + (step * buoyancy) * centre[3]
        out.append(total)
    return out, centre


def forcing_of(parts, count):
    total = jnp.sum(parts[...])
    return (target_speed - total / count) / relax_time


def first_kernel(count, tiles, flags, coefs, fields, left, right, plane, drag, sums, section, partial, state):
    width, span, levels = fields.shape[1:]
    is_first = flags[0] == 0
    is_last = flags[0] == tiles - 1
    rows = pl.ds(SUB, span)

    for f in range(4):

        @pl.loop(0, width)
        def _(i):
            state[f, i + 6, rows, :] = fields[f, i]

        @pl.when(jnp.logical_not(is_first))
        def _():
            for i in range(6):
                state[f, i, rows, :] = left[f, i]

        @pl.when(is_first)
        def _():
            for i in range(3):
                state[f, i, rows, :] = plane[3 * f + i]
                state[f, i + 3, rows, :] = plane[3 * f + i]

        @pl.when(jnp.logical_not(is_last))
        def _():
            for i in range(6):
                state[f, width + 6 + i, rows, :] = right[f, i]

        @pl.when(is_last)
        def _():
            for i in range(6):
                state[f, width + 6 + i, rows, :] = fields[f, width - 1]

        @pl.loop(0, width + 12)
        def _(i):
            wrap_rows(state, f, i, span)

    added = FIRST * forcing_of(sums, count)
    surface = coefs[0]
    partial[...] = jnp.zeros_like(partial)

    @pl.loop(0, width + 6)
    def _(layer):
        own = jnp.logical_and(layer >= 3, layer < width + 3).astype(jnp.float32)
        for chunk in range(span // SUB):
            change, centre = stage_chunk(
                state, layer, chunk, FIRST, FIRST * drag[layer, pl.ds(SUB * chunk, SUB), :], FIRST * surface, levels
            )
            for f in range(4):
                value = centre[f] + change[f]
                if f == 0:
                    value = value + added
                    partial[...] += own * value
                section[f, layer, pl.ds(SUB + SUB * chunk, SUB), :] = value
        for f in range(4):
            wrap_rows(section, f, layer, span)

    @pl.when(is_first)
    def _():
        for f in range(4):
            for i in range(3):
                section[f, i] = state[f, i + 3]

    @pl.when(is_last)
    def _():
        for f in range(4):
            for i in range(3):
                section[f, width + 3 + i] = section[f, width + 2]


def second_kernel(coefs, fields, section, drag, out):
    width, span, levels = fields.shape[1:]
    surface = coefs[0]

    @pl.loop(0, width)
    def _(layer):
        for chunk in range(span // SUB):
            rows = pl.ds(SUB * chunk, SUB)
            change, _ = stage_chunk(
                section, layer, chunk, SECOND, SECOND * drag[layer + 3, rows, :], SECOND * surface, levels
            )
            for f in range(4):
                out[f, layer, rows, :] = fields[f, layer, rows, :] + change[f]


def last_kernel(count, sums, before, out):
    added = SECOND * forcing_of(sums, count)
    out[...] = before[...] + added


def coefficients(indices, drag_table, rough_table):
    slots = jnp.arange(drag_table.shape[0], dtype=jnp.int32)
    drag_coef = jnp.sum(jnp.where(slots == indices[0], drag_table, 0.0))
    rough = jnp.sum(jnp.where(slots == indices[1], rough_table, 0.0))
    surface_coef = (karman / jnp.log(0.5 * spacing / rough)) ** 2
    return (drag_coef, surface_coef)


def local(fields, precursor, heights, param_index, drag_table, rough_table):
    state = fields[0]
    width, span, levels = state.shape[1:]
    tiles = lax.axis_size("gx")
    members = lax.axis_size("mem")
    tile = lax.axis_index("gx")
    count = tiles * width * span * levels
    vmem = pl.BlockSpec(memory_space=pltpu.VMEM)
    smem = pl.BlockSpec(memory_space=pltpu.SMEM)
    f32 = jnp.float32

    ends = tiles - 1
    left = lax.ppermute(state[:, width - 6 :], "gx", [(i, i + 1) for i in range(ends)])
    right = lax.ppermute(state[:, :6], "gx", [(i + 1, i) for i in range(ends)])

    piece = precursor.size
    shards = jnp.broadcast_to(precursor.reshape(1, 1, piece), (members, 1, piece))
    gathered = lax.all_to_all(shards, "mem", 0, 0, tiled=True)
    plane = gathered.reshape(members, 12, piece // 12).transpose(1, 0, 2).reshape(12, span, levels)

    own = jnp.sum(state[0].reshape(-1, SUB, levels), axis=0)
    sums = lax.all_to_all(jnp.broadcast_to(own[None], (tiles, SUB, levels)), "gx", 0, 0, tiled=True)

    drag_coef, surface_coef = coefficients(param_index[0], drag_table, rough_table)
    padded_heights = jnp.pad(heights, ((3, 3), (0, 0)), mode="edge")
    columns = lax.dynamic_slice_in_dim(padded_heights, tile * width, width + 6, 0)
    level = lax.broadcasted_iota(jnp.int32, (width + 6, span, levels), 2)
    drag = jnp.where(level < columns[:, :, None], drag_coef, 0.0)
    coefs = (surface_coef / spacing).reshape(1)
    flags = tile.astype(jnp.int32).reshape(1)

    section, partial = pl.pallas_call(
        functools.partial(first_kernel, count, tiles),
        out_shape=(
            jax.ShapeDtypeStruct((4, width + 6, span + 2 * SUB, levels), f32),
            jax.ShapeDtypeStruct((SUB, levels), f32),
        ),
        in_specs=[smem, smem] + [vmem] * 6,
        out_specs=(vmem, vmem),
        scratch_shapes=[pltpu.VMEM((4, width + 12, span + 2 * SUB, levels), f32)],
        compiler_params=pltpu.CompilerParams(vmem_limit_bytes=24 * 2**20),
        cost_estimate=pl.CostEstimate(flops=20_000_000, bytes_accessed=6_000_000, transcendentals=0),
        name="first_stage",
    )(flags, coefs, state, left, right, plane, drag, sums)

    later = lax.all_to_all(jnp.broadcast_to(partial[None], (tiles, SUB, levels)), "gx", 0, 0, tiled=True)

    before = pl.pallas_call(
        second_kernel,
        out_shape=jax.ShapeDtypeStruct(state.shape, f32),
        in_specs=[smem] + [vmem] * 3,
        out_specs=vmem,
        compiler_params=pltpu.CompilerParams(vmem_limit_bytes=24 * 2**20),
        cost_estimate=pl.CostEstimate(flops=20_000_000, bytes_accessed=6_000_000, transcendentals=0),
        name="second_stage",
    )(coefs, state, section, drag)

    block = pl.BlockSpec((1, width, span, levels), lambda i: (0, 0, 0, 0))
    out = pl.pallas_call(
        functools.partial(last_kernel, count),
        grid=(1,),
        out_shape=jax.ShapeDtypeStruct(state.shape, f32),
        in_specs=[pl.BlockSpec((tiles, SUB, levels), lambda i: (0, 0, 0)), block],
        out_specs=block,
        input_output_aliases={1: 0},
        name="add_forcing",
    )(later, before)
    return out[None]


def solution(mesh):
    in_specs = (P("mem", None, "gx", None, None), P(None, "mem"), P(), P("mem", None), P(), P())
    out_specs = P("mem", None, "gx", None, None)
    return jax.shard_map(local, mesh=mesh, in_specs=in_specs, out_specs=out_specs, check_vma=False)
```

```python
import functools

import jax
import jax.numpy as jnp
from jax import lax
from jax.experimental import pallas as pl
from jax.experimental.pallas import tpu as pltpu
from jax.sharding import PartitionSpec as P

spacing = 2.0
time_step = 0.2
viscosity = 1.0
target_speed = 3.0
relax_time = 1.0
karman = 0.4
buoyancy = 0.0327

SUB = 8
REACH = 3
HALO = 2 * REACH
FIRST = time_step / 3.0
SECOND = time_step / 2.0
SHARD_ROWS = 64

SECTION_AT = 8
EIGHTH_AT = 16


def wrap_rows(ref, field, layer, span):
    ref[field, layer, pl.ds(SUB - REACH, REACH), :] = ref[field, layer, pl.ds(SUB + span - REACH, REACH), :]
    ref[field, layer, pl.ds(SUB + span, REACH), :] = ref[field, layer, pl.ds(SUB, REACH), :]


def direction(speed, step):
    slow = speed * (step / (60.0 * spacing))
    size = jnp.abs(slow)
    near = 15.0 * size + step * viscosity / (spacing * spacing)
    wide = 45.0 * slow
    odd = 9.0 * slow
    even = 6.0 * size
    weights = {
        1: near - wide,
        -1: near + wide,
        2: odd - even,
        -2: -(odd + even),
        3: size - slow,
        -3: size + slow,
    }
    return weights, 20.0 * size


def stage_chunk(state, layer, chunk, step, drag, surface, levels):
    row = SUB + SUB * chunk

    def load(field, dx, dy):
        return state[field, layer + REACH + dx, pl.ds(row + dy, SUB), :]

    centre = [load(f, 0, 0) for f in range(4)]
    u, v, w = centre[:3]
    diffuse = step * viscosity / (spacing * spacing)
    along_x, mid_x = direction(u, step)
    along_y, mid_y = direction(v, step)
    lane = lax.broadcasted_iota(jnp.int32, u.shape, 1)
    lift = w * (step / (2.0 * spacing))
    up = jnp.where(lane == levels - 1, 0.0, diffuse - lift)
    down = jnp.where(lane == 0, 0.0, diffuse + lift)
    speed = step * jnp.sqrt(u * u + v * v + w * w)
    middle = -(mid_x + mid_y + 6.0 * diffuse + speed * drag)
    middle_uv = middle - jnp.where(lane == 0, speed * surface, 0.0)
    out = []
    for f in range(4):
        s = centre[f]
        total = (middle_uv if f < 2 else middle) * s
        total = total + up * pltpu.roll(s, levels - 1, 1) + down * pltpu.roll(s, 1, 1)
        for k in (1, -1, 2, -2, 3, -3):
            total = total + along_x[k] * load(f, k, 0)
            total = total + along_y[k] * load(f, 0, k)
        if f == 2:
            total = total + (step * buoyancy) * centre[3]
        out.append(total)
    return out, centre


def from_inlet(u, layer, planes):
    along, _ = direction(u, FIRST)
    total = None
    for p in range(layer, REACH):
        term = along[p - REACH - layer] * planes[p]
        total = term if total is None else total + term
    return total


def forcing_of(total, count):
    return (target_speed - jnp.sum(total) / count) / relax_time


def total_of(ref, at):
    total = ref[0, pl.ds(at, SUB), :]
    for g in range(1, ref.shape[0]):
        total = total + ref[g, pl.ds(at, SUB), :]
    return total


def edges_kernel(fields, head, tail, state, sems):
    width = fields.shape[1]
    copies = [
        pltpu.make_async_copy(fields, state, sems.at[2]),
        pltpu.make_async_copy(fields.at[:, pl.ds(0, HALO)], head, sems.at[0]),
        pltpu.make_async_copy(fields.at[:, pl.ds(width - HALO, HALO)], tail, sems.at[1]),
    ]
    for copy in copies:
        copy.start()
    for copy in copies:
        copy.wait()


def inner_kernel(
    place, index, drag_table, rough_table, heights, fields, section, drag, surface, partial, sums, state, picks, drags, roughs, tops, sems
):
    width, span, levels = fields.shape[1:]
    copies = [
        pltpu.make_async_copy(source, target, sems.at[k])
        for k, (source, target) in enumerate(
            ((index, picks), (drag_table, drags), (rough_table, roughs), (heights, tops))
        )
    ]
    for copy in copies:
        copy.start()

    for f in range(4):

        @pl.loop(0, width, unroll=4)
        def _(i):
            state[f, i, pl.ds(SUB, span), :] = fields[f, i]
            wrap_rows(state, f, i, span)

    for copy in copies:
        copy.wait()
    rough = jnp.full((SUB, levels), roughs[picks[0, 1]], jnp.float32)
    ratio = karman / jnp.log(0.5 * spacing / rough)
    surface[...] = ratio * ratio / spacing
    coef = drags[picks[0, 0]]
    columns = tops.shape[1]
    level = lax.broadcasted_iota(jnp.int32, (span, levels), 1)
    here = pltpu.roll(tops[...], lax.rem(columns - place[0] * width, columns), 1)
    is_first = place[0] == 0
    is_last = (place[0] + 1) * width == columns
    for layer in range(-REACH, width + REACH):
        column = here[:, layer % columns : layer % columns + 1]
        if layer < 0:
            column = jnp.where(is_first, here[:, 0:1], column)
        if layer >= width:
            column = jnp.where(is_last, here[:, width - 1 : width], column)
        drag[layer + REACH] = jnp.where(level < column, coef, 0.0)

    total = [jnp.zeros(sums.shape, jnp.float32) for _ in range(4)]
    for layer in range(width):
        for c in range(span // SUB):
            total[c % 4] = total[c % 4] + fields[0, layer, pl.ds(SUB * c, SUB), :]
    sums[...] = (total[0] + total[1]) + (total[2] + total[3])
    partial[...] = jnp.zeros_like(partial)

    @pl.loop(0, width - HALO)
    def _(layer):
        at = layer + HALO
        for chunk in range(span // SUB):
            rows = pl.ds(SUB * chunk, SUB)
            change, centre = stage_chunk(state, layer, chunk, FIRST, drag[at, rows, :], surface[...], levels)
            for f in range(4):
                value = centre[f] + change[f]
                if f == 0:
                    partial[...] += value
                section[f, at, pl.ds(SUB + SUB * chunk, SUB), :] = value
        for f in range(4):
            wrap_rows(section, f, at, span)


def outer_kernel(tiles, place, drag, surface, fields, left, right, before, inner, section, sums, low, high):
    width, span, levels = fields.shape[1:]
    is_last = place[0] == tiles - 1
    rows = pl.ds(SUB, span)
    full = section.shape[1]

    for f in range(4):

        @pl.loop(0, HALO, unroll=True)
        def _(i):
            low[f, i, rows, :] = left[f, i]
            low[f, HALO + i, rows, :] = fields[f, i]
            high[f, i, rows, :] = fields[f, width - HALO + i]
            high[f, HALO + i, rows, :] = jnp.where(is_last, fields[f, width - 1], right[f, i])
            for ref in (low, high):
                wrap_rows(ref, f, i, span)
                wrap_rows(ref, f, HALO + i, span)

    sums[...] = inner[...]

    for ref, first_at, own in ((low, 0, (REACH, HALO)), (high, full - HALO, (0, REACH))):

        @pl.loop(0, HALO)
        def _(layer):
            at = first_at + layer
            mine = jnp.logical_and(layer >= own[0], layer < own[1]).astype(jnp.float32)
            for chunk in range(span // SUB):
                lines = pl.ds(SUB * chunk, SUB)
                change, centre = stage_chunk(ref, layer, chunk, FIRST, drag[at, lines, :], surface[...], levels)
                for f in range(4):
                    value = centre[f] + change[f]
                    if f == 0:
                        sums[...] += mine * value
                    section[f, at, pl.ds(SUB + SUB * chunk, SUB), :] = value
            for f in range(4):
                wrap_rows(section, f, at, span)

    @pl.when(is_last)
    def _():
        for f in range(4):
            for i in range(REACH):
                section[f, full - REACH + i] = section[f, full - REACH - 1]


def regroup_kernel(shards, eighth):
    per = shards.shape[0] // 2
    count = eighth.shape[0] // per
    for y in range(per):
        low, high = (shards[2 * y + h, pl.ds(0, count), :] for h in (0, 1))
        eighth[pl.ds(y, count, stride=per), :] = low + pltpu.roll(high, eighth.shape[1] // 2, 1)


def pack_kernel(first, second, fields, eighth, message):
    tiles = message.shape[0]
    span = fields.shape[2]
    lead_at = EIGHTH_AT + eighth.shape[0]
    for d in range(tiles):
        message[d, pl.ds(0, SUB), :] = first[...]
        message[d, pl.ds(SECTION_AT, SUB), :] = second[...]
        message[d, pl.ds(EIGHTH_AT, eighth.shape[0]), :] = eighth[...]
        for i in range(REACH):
            message[d, pl.ds(lead_at + span * i, span), :] = fields[0, i]


def second_kernel(
    count, place, drag, surface, fields, before, received, out, section, planes, result, sems
):
    tiles = received.shape[0]
    width, span, levels = fields.shape[1:]
    per = span // tiles
    lead_at = received.shape[1] - REACH * span
    is_first = place[0] == 0

    def assemble(r):
        for g in range(tiles):
            planes[r, pl.ds(per * g, per), :] = received[g, pl.ds(EIGHTH_AT + per * r, per), :]

    for r in range(REACH):
        assemble(r)
    extra = total_of(received, SECTION_AT)
    for c in range(span // SUB):
        rows = pl.ds(SUB * c, SUB)
        for i in range(REACH):
            lead = received[0, pl.ds(lead_at + span * i + SUB * c, SUB), :]
            extra = extra + from_inlet(lead, i, [planes[p, rows, :] for p in range(REACH)])
    added = FIRST * forcing_of(total_of(received, 0), count)
    forcing = SECOND * (forcing_of(extra, count) - added / relax_time)

    @pl.loop(0, section.shape[1], unroll=2)
    def _(at):
        section[0, at] = before[0, at] + added

    @pl.when(is_first)
    def _():
        for r in range(REACH, planes.shape[0]):
            assemble(r)
        for f in range(4):
            for i in range(REACH):
                section[f, i, pl.ds(SUB, span), :] = planes[REACH * f + i]
                section[f, REACH + i, pl.ds(SUB, span), :] += from_inlet(
                    fields[0, i], i, [planes[REACH * f + p] for p in range(REACH)]
                )
            for i in range(HALO):
                wrap_rows(section, f, i, span)

    copies = []
    step = width // sems.shape[0]
    for k in range(sems.shape[0]):

        @pl.loop(step * k, step * (k + 1))
        def _(layer):
            for chunk in range(span // SUB):
                rows = pl.ds(SUB * chunk, SUB)
                change, _ = stage_chunk(
                    section, layer, chunk, SECOND, drag[layer + REACH, rows, :], surface[...], levels
                )
                for f in range(4):
                    value = fields[f, layer, rows, :] + change[f]
                    if f == 0:
                        value = value + forcing
                    result[f, layer, rows, :] = value

        layers = pl.ds(step * k, step)
        copies.append(pltpu.make_async_copy(result.at[:, layers], out.at[:, layers], sems.at[k]))
        copies[-1].start()
    for copy in copies:
        copy.wait()


def local(fields, precursor, heights, param_index, drag_table, rough_table):
    state = fields[0]
    width, span, levels = state.shape[1:]
    tiles = lax.axis_size("gx")
    members = lax.axis_size("mem")
    tile = lax.axis_index("gx").astype(jnp.int32).reshape(1)
    count = tiles * width * span * levels
    f32 = jnp.float32
    vmem = pl.BlockSpec(memory_space=pltpu.VMEM)
    smem = pl.BlockSpec(memory_space=pltpu.SMEM)
    whole = pl.BlockSpec(memory_space=pl.ANY)
    tall = span + 2 * SUB
    full = width + HALO
    shape = jax.ShapeDtypeStruct
    params = pltpu.CompilerParams(vmem_limit_bytes=8 * 2**20)
    tile_sum = shape((SUB, levels), f32)

    blocks = members // tiles
    deal = [
        ((tiles * g + j) * tiles + b, (tiles * b + j) * tiles + g)
        for b in range(blocks)
        for j in range(tiles)
        for g in range(tiles)
    ]
    groups = [[tiles * b + j for j in range(tiles)] for b in range(blocks)]
    half = jnp.pad(precursor, ((0, SHARD_ROWS - precursor.shape[0]), (0, levels - precursor.shape[1])))
    shards = lax.all_to_all(
        jnp.broadcast_to(half[None], (tiles,) + half.shape), "mem", 0, 0, tiled=True, axis_index_groups=groups
    )
    eighth = pl.pallas_call(
        regroup_kernel,
        out_shape=shape((precursor.shape[0] * span // tiles, levels), f32),
        in_specs=[vmem],
        out_specs=vmem,
        compiler_params=pltpu.CompilerParams(vmem_limit_bytes=2 * 2**20),
        name="regroup",
    )(shards)
    eighth = lax.ppermute(eighth, ("mem", "gx"), deal)

    hbm = functools.partial(pltpu.with_memory_space_constraint, memory_space=pltpu.HBM)
    head, tail, state = pl.pallas_call(
        edges_kernel,
        out_shape=(shape((4, HALO, span, levels), f32), shape((4, HALO, span, levels), f32), shape(state.shape, f32)),
        in_specs=[whole],
        out_specs=(whole, whole, vmem),
        scratch_shapes=[pltpu.SemaphoreType.DMA((3,))],
        compiler_params=pltpu.CompilerParams(vmem_limit_bytes=4 * 2**20),
        name="edges",
    )(hbm(state))
    ends = tiles - 1
    left = lax.ppermute(tail, "gx", [(i, i + 1) for i in range(ends)])
    right = lax.ppermute(head, "gx", [(i + 1, i) for i in range(ends)])

    before, drag, surface, inner_sum, sums = pl.pallas_call(
        inner_kernel,
        out_shape=(
            shape((4, full, tall, levels), f32),
            shape((full, span, levels), f32),
            tile_sum,
            tile_sum,
            tile_sum,
        ),
        in_specs=[smem] + [whole] * 4 + [vmem],
        out_specs=(vmem,) * 5,
        scratch_shapes=[
            pltpu.VMEM((4, width, tall, levels), f32),
            pltpu.SMEM(param_index.shape, jnp.int32),
            pltpu.SMEM(drag_table.shape, f32),
            pltpu.SMEM(rough_table.shape, f32),
            pltpu.VMEM((span, heights.shape[0]), jnp.int32),
            pltpu.SemaphoreType.DMA((4,)),
        ],
        compiler_params=params,
        cost_estimate=pl.CostEstimate(flops=10_000_000, bytes_accessed=4_000_000, transcendentals=0),
        name="inner",
    )(tile, hbm(param_index), hbm(drag_table), hbm(rough_table), hbm(heights.T), state)

    section, outer_sum = pl.pallas_call(
        functools.partial(outer_kernel, tiles),
        out_shape=(shape((4, full, tall, levels), f32), tile_sum),
        in_specs=[smem] + [vmem] * 7,
        out_specs=(vmem, vmem),
        scratch_shapes=[
            pltpu.VMEM((4, 2 * HALO, tall, levels), f32),
            pltpu.VMEM((4, 2 * HALO, tall, levels), f32),
        ],
        input_output_aliases={6: 0},
        compiler_params=params,
        cost_estimate=pl.CostEstimate(flops=12_000_000, bytes_accessed=4_000_000, transcendentals=0),
        name="outer",
    )(tile, drag, surface, state, left, right, before, inner_sum)

    message = pl.pallas_call(
        pack_kernel,
        out_shape=shape((tiles, EIGHTH_AT + eighth.shape[0] + REACH * span, levels), f32),
        in_specs=[vmem] * 4,
        out_specs=vmem,
        compiler_params=params,
        name="pack",
    )(sums, outer_sum, state, eighth)
    received = lax.all_to_all(message, "gx", 0, 0, tiled=True)

    out, _ = pl.pallas_call(
        functools.partial(second_kernel, count),
        out_shape=(shape(state.shape, f32), shape(section.shape, f32)),
        in_specs=[smem] + [vmem] * 5,
        out_specs=(whole, vmem),
        scratch_shapes=[
            pltpu.VMEM((precursor.shape[0], span, levels), f32),
            pltpu.VMEM(state.shape, f32),
            pltpu.SemaphoreType.DMA((4,)),
        ],
        input_output_aliases={4: 1},
        compiler_params=params,
        name="second",
    )(tile, drag, surface, state, section, received)
    return out[None]


def solution(mesh):
    in_specs = (P("mem", None, "gx", None, None), P(None, "mem"), P(), P("mem", None), P(), P())
    out_specs = P("mem", None, "gx", None, None)
    return jax.shard_map(local, mesh=mesh, in_specs=in_specs, out_specs=out_specs, check_vma=False)
```

```python
import functools

import jax
import jax.numpy as jnp
from jax import lax
from jax.experimental import pallas as pl
from jax.experimental.pallas import tpu as pltpu
from jax.sharding import PartitionSpec as P

spacing = 2.0
time_step = 0.2
viscosity = 1.0
target_speed = 3.0
relax_time = 1.0
karman = 0.4
buoyancy = 0.0327

SUB = 8
REACH = 3
HALO = 2 * REACH
FIRST = time_step / 3.0
SECOND = time_step / 2.0
SHARD_ROWS = 56

SECTION_AT = 8
EIGHTH_AT = 16


def wrap_rows(ref, field, layer, span):
    ref[field, layer, pl.ds(SUB - REACH, REACH), :] = ref[field, layer, pl.ds(SUB + span - REACH, REACH), :]
    ref[field, layer, pl.ds(SUB + span, REACH), :] = ref[field, layer, pl.ds(SUB, REACH), :]


def direction(speed, step):
    slow = speed * (step / (60.0 * spacing))
    size = jnp.abs(slow)
    near = 15.0 * size + step * viscosity / (spacing * spacing)
    wide = 45.0 * slow
    odd = 9.0 * slow
    even = 6.0 * size
    weights = {
        1: near - wide,
        -1: near + wide,
        2: odd - even,
        -2: -(odd + even),
        3: size - slow,
        -3: size + slow,
    }
    return weights, 20.0 * size


def stage_chunk(state, layer, chunk, step, drag, surface, levels):
    row = SUB + SUB * chunk

    def load(field, dx, dy):
        return state[field, layer + REACH + dx, pl.ds(row + dy, SUB), :]

    centre = [load(f, 0, 0) for f in range(4)]
    u, v, w = centre[:3]
    diffuse = step * viscosity / (spacing * spacing)
    along_x, mid_x = direction(u, step)
    along_y, mid_y = direction(v, step)
    lane = lax.broadcasted_iota(jnp.int32, u.shape, 1)
    lift = w * (step / (2.0 * spacing))
    up = jnp.where(lane == levels - 1, 0.0, diffuse - lift)
    down = jnp.where(lane == 0, 0.0, diffuse + lift)
    speed = step * jnp.sqrt(u * u + v * v + w * w)
    middle = -(mid_x + mid_y + 6.0 * diffuse + speed * drag)
    middle_uv = middle - jnp.where(lane == 0, speed * surface, 0.0)
    out = []
    for f in range(4):
        s = centre[f]
        total = (middle_uv if f < 2 else middle) * s
        total = total + up * pltpu.roll(s, levels - 1, 1) + down * pltpu.roll(s, 1, 1)
        for k in (1, -1, 2, -2, 3, -3):
            total = total + along_x[k] * load(f, k, 0)
            total = total + along_y[k] * load(f, 0, k)
        if f == 2:
            total = total + (step * buoyancy) * centre[3]
        out.append(total)
    return out, centre


def from_inlet(u, layer, planes):
    along, _ = direction(u, FIRST)
    total = None
    for p in range(layer, REACH):
        term = along[p - REACH - layer] * planes[p]
        total = term if total is None else total + term
    return total


def forcing_of(total, count):
    return (target_speed - jnp.sum(total) / count) / relax_time


def total_of(ref, at):
    total = ref[0, pl.ds(at, SUB), :]
    for g in range(1, ref.shape[0]):
        total = total + ref[g, pl.ds(at, SUB), :]
    return total


def edges_kernel(fields, precursor, head, tail, state, message, shard, padded, sems):
    width = fields.shape[1]
    rows, lanes = shard.shape
    copies = [
        pltpu.make_async_copy(precursor, shard, sems.at[3]),
        pltpu.make_async_copy(fields, state, sems.at[2]),
        pltpu.make_async_copy(fields.at[:, pl.ds(0, HALO)], head, sems.at[0]),
        pltpu.make_async_copy(fields.at[:, pl.ds(width - HALO, HALO)], tail, sems.at[1]),
    ]
    for copy in copies:
        copy.start()
    padded[...] = jnp.zeros_like(padded)
    copies[0].wait()
    padded[pl.ds(0, rows), pl.ds(0, lanes)] = shard[...]
    for d in range(message.shape[0]):
        copy = pltpu.make_async_copy(padded, message.at[d, pl.ds(0, padded.shape[0])], sems.at[4 + d])
        copy.start()
        copies.append(copy)
    for copy in copies[1:]:
        copy.wait()


def inner_kernel(
    place, index, drag_table, rough_table, heights, fields, section, drag, surface, partial, sums, state, picks, drags, roughs, tops, sems
):
    width, span, levels = fields.shape[1:]
    copies = [
        pltpu.make_async_copy(source, target, sems.at[k])
        for k, (source, target) in enumerate(
            ((index, picks), (drag_table, drags), (rough_table, roughs), (heights, tops))
        )
    ]
    for copy in copies:
        copy.start()

    for f in range(4):

        @pl.loop(0, width, unroll=4)
        def _(i):
            state[f, i, pl.ds(SUB, span), :] = fields[f, i]
            wrap_rows(state, f, i, span)

    for copy in copies:
        copy.wait()
    rough = jnp.full((SUB, levels), roughs[picks[0, 1]], jnp.float32)
    ratio = karman / jnp.log(0.5 * spacing / rough)
    surface[...] = ratio * ratio / spacing
    coef = drags[picks[0, 0]]
    columns = tops.shape[1]
    level = lax.broadcasted_iota(jnp.int32, (span, levels), 1)
    here = pltpu.roll(tops[...], lax.rem(columns - place[0] * width, columns), 1)
    is_first = place[0] == 0
    is_last = (place[0] + 1) * width == columns
    for layer in range(-REACH, width + REACH):
        column = here[:, layer % columns : layer % columns + 1]
        if layer < 0:
            column = jnp.where(is_first, here[:, 0:1], column)
        if layer >= width:
            column = jnp.where(is_last, here[:, width - 1 : width], column)
        drag[layer + REACH] = jnp.where(level < column, coef, 0.0)

    total = [jnp.zeros(sums.shape, jnp.float32) for _ in range(4)]
    for layer in range(width):
        for c in range(span // SUB):
            total[c % 4] = total[c % 4] + fields[0, layer, pl.ds(SUB * c, SUB), :]
    sums[...] = (total[0] + total[1]) + (total[2] + total[3])
    partial[...] = jnp.zeros_like(partial)

    @pl.loop(0, width - HALO)
    def _(layer):
        at = layer + HALO
        for chunk in range(span // SUB):
            rows = pl.ds(SUB * chunk, SUB)
            change, centre = stage_chunk(state, layer, chunk, FIRST, drag[at, rows, :], surface[...], levels)
            for f in range(4):
                value = centre[f] + change[f]
                if f == 0:
                    partial[...] += value
                section[f, at, pl.ds(SUB + SUB * chunk, SUB), :] = value
        for f in range(4):
            wrap_rows(section, f, at, span)


def outer_kernel(tiles, place, drag, surface, fields, left, right, before, inner, section, sums, low, high):
    width, span, levels = fields.shape[1:]
    is_last = place[0] == tiles - 1
    rows = pl.ds(SUB, span)
    full = section.shape[1]

    for f in range(4):

        @pl.loop(0, HALO, unroll=True)
        def _(i):
            low[f, i, rows, :] = left[f, i]
            low[f, HALO + i, rows, :] = fields[f, i]
            high[f, i, rows, :] = fields[f, width - HALO + i]
            high[f, HALO + i, rows, :] = jnp.where(is_last, fields[f, width - 1], right[f, i])
            for ref in (low, high):
                wrap_rows(ref, f, i, span)
                wrap_rows(ref, f, HALO + i, span)

    sums[...] = inner[...]

    for ref, first_at, own in ((low, 0, (REACH, HALO)), (high, full - HALO, (0, REACH))):

        @pl.loop(0, HALO)
        def _(layer):
            at = first_at + layer
            mine = jnp.logical_and(layer >= own[0], layer < own[1]).astype(jnp.float32)
            for chunk in range(span // SUB):
                lines = pl.ds(SUB * chunk, SUB)
                change, centre = stage_chunk(ref, layer, chunk, FIRST, drag[at, lines, :], surface[...], levels)
                for f in range(4):
                    value = centre[f] + change[f]
                    if f == 0:
                        sums[...] += mine * value
                    section[f, at, pl.ds(SUB + SUB * chunk, SUB), :] = value
            for f in range(4):
                wrap_rows(section, f, at, span)

    @pl.when(is_last)
    def _():
        for f in range(4):
            for i in range(REACH):
                section[f, full - REACH + i] = section[f, full - REACH - 1]


def regroup_kernel(shards, eighth):
    per = shards.shape[0] // 2
    count = eighth.shape[0] // per
    for y in range(per):
        low, high = (shards[2 * y + h, pl.ds(0, count), :] for h in (0, 1))
        eighth[pl.ds(y, count, stride=per), :] = low + pltpu.roll(high, eighth.shape[1] // 2, 1)


def pack_kernel(first, second, fields, eighth, message):
    tiles = message.shape[0]
    span = fields.shape[2]
    lead_at = EIGHTH_AT + eighth.shape[0]
    for d in range(tiles):
        message[d, pl.ds(0, SUB), :] = first[...]
        message[d, pl.ds(SECTION_AT, SUB), :] = second[...]
        message[d, pl.ds(EIGHTH_AT, eighth.shape[0]), :] = eighth[...]
        for i in range(REACH):
            message[d, pl.ds(lead_at + span * i, span), :] = fields[0, i]


def second_kernel(
    count, place, drag, surface, fields, before, received, out, section, planes, result, sems
):
    tiles = received.shape[0]
    width, span, levels = fields.shape[1:]
    per = span // tiles
    lead_at = received.shape[1] - REACH * span
    is_first = place[0] == 0

    def assemble(r):
        for g in range(tiles):
            planes[r, pl.ds(per * g, per), :] = received[g, pl.ds(EIGHTH_AT + per * r, per), :]

    for r in range(REACH):
        assemble(r)
    extra = total_of(received, SECTION_AT)
    for c in range(span // SUB):
        rows = pl.ds(SUB * c, SUB)
        for i in range(REACH):
            lead = received[0, pl.ds(lead_at + span * i + SUB * c, SUB), :]
            extra = extra + from_inlet(lead, i, [planes[p, rows, :] for p in range(REACH)])
    added = FIRST * forcing_of(total_of(received, 0), count)
    forcing = SECOND * (forcing_of(extra, count) - added / relax_time)

    @pl.loop(0, section.shape[1], unroll=2)
    def _(at):
        section[0, at] = before[0, at] + added

    @pl.when(is_first)
    def _():
        for r in range(REACH, planes.shape[0]):
            assemble(r)
        for f in range(4):
            for i in range(REACH):
                section[f, i, pl.ds(SUB, span), :] = planes[REACH * f + i]
                section[f, REACH + i, pl.ds(SUB, span), :] += from_inlet(
                    fields[0, i], i, [planes[REACH * f + p] for p in range(REACH)]
                )
            for i in range(HALO):
                wrap_rows(section, f, i, span)

    copies = []
    step = width // sems.shape[0]
    for k in range(sems.shape[0]):

        @pl.loop(step * k, step * (k + 1))
        def _(layer):
            for chunk in range(span // SUB):
                rows = pl.ds(SUB * chunk, SUB)
                change, _ = stage_chunk(
                    section, layer, chunk, SECOND, drag[layer + REACH, rows, :], surface[...], levels
                )
                for f in range(4):
                    value = fields[f, layer, rows, :] + change[f]
                    if f == 0:
                        value = value + forcing
                    result[f, layer, rows, :] = value

        layers = pl.ds(step * k, step)
        copies.append(pltpu.make_async_copy(result.at[:, layers], out.at[:, layers], sems.at[k]))
        copies[-1].start()
    for copy in copies:
        copy.wait()


def local(fields, precursor, heights, param_index, drag_table, rough_table):
    state = fields[0]
    width, span, levels = state.shape[1:]
    tiles = lax.axis_size("gx")
    members = lax.axis_size("mem")
    tile = lax.axis_index("gx").astype(jnp.int32).reshape(1)
    count = tiles * width * span * levels
    f32 = jnp.float32
    vmem = pl.BlockSpec(memory_space=pltpu.VMEM)
    smem = pl.BlockSpec(memory_space=pltpu.SMEM)
    whole = pl.BlockSpec(memory_space=pl.ANY)
    tall = span + 2 * SUB
    full = width + HALO
    shape = jax.ShapeDtypeStruct
    params = pltpu.CompilerParams(vmem_limit_bytes=8 * 2**20)
    tile_sum = shape((SUB, levels), f32)

    blocks = members // tiles
    deal = [
        ((tiles * g + j) * tiles + b, (tiles * b + j) * tiles + g)
        for b in range(blocks)
        for j in range(tiles)
        for g in range(tiles)
    ]
    groups = [[tiles * b + j for j in range(tiles)] for b in range(blocks)]
    hbm = functools.partial(pltpu.with_memory_space_constraint, memory_space=pltpu.HBM)
    head, tail, state, message = pl.pallas_call(
        edges_kernel,
        out_shape=(
            shape((4, HALO, span, levels), f32),
            shape((4, HALO, span, levels), f32),
            shape(state.shape, f32),
            shape((tiles, SHARD_ROWS, levels), f32),
        ),
        in_specs=[whole, whole],
        out_specs=(vmem, vmem, vmem, whole),
        scratch_shapes=[
            pltpu.VMEM(precursor.shape, f32),
            pltpu.VMEM((2 * SUB, levels), f32),
            pltpu.SemaphoreType.DMA((4 + tiles,)),
        ],
        compiler_params=pltpu.CompilerParams(vmem_limit_bytes=4 * 2**20),
        name="edges",
    )(hbm(state), hbm(precursor))
    shards = lax.all_to_all(message, "mem", 0, 0, tiled=True, axis_index_groups=groups)
    eighth = pl.pallas_call(
        regroup_kernel,
        out_shape=shape((precursor.shape[0] * span // tiles, levels), f32),
        in_specs=[vmem],
        out_specs=vmem,
        compiler_params=pltpu.CompilerParams(vmem_limit_bytes=2 * 2**20),
        name="regroup",
    )(shards)
    eighth = lax.ppermute(eighth, ("mem", "gx"), deal)

    ends = tiles - 1
    left = lax.ppermute(tail, "gx", [(i, i + 1) for i in range(ends)])
    right = lax.ppermute(head, "gx", [(i + 1, i) for i in range(ends)])

    before, drag, surface, inner_sum, sums = pl.pallas_call(
        inner_kernel,
        out_shape=(
            shape((4, full, tall, levels), f32),
            shape((full, span, levels), f32),
            tile_sum,
            tile_sum,
            tile_sum,
        ),
        in_specs=[smem] + [whole] * 4 + [vmem],
        out_specs=(vmem,) * 5,
        scratch_shapes=[
            pltpu.VMEM((4, width, tall, levels), f32),
            pltpu.SMEM(param_index.shape, jnp.int32),
            pltpu.SMEM(drag_table.shape, f32),
            pltpu.SMEM(rough_table.shape, f32),
            pltpu.VMEM((span, heights.shape[0]), jnp.int32),
            pltpu.SemaphoreType.DMA((4,)),
        ],
        compiler_params=params,
        cost_estimate=pl.CostEstimate(flops=10_000_000, bytes_accessed=4_000_000, transcendentals=0),
        name="inner",
    )(tile, hbm(param_index), hbm(drag_table), hbm(rough_table), hbm(heights.T), state)

    section, outer_sum = pl.pallas_call(
        functools.partial(outer_kernel, tiles),
        out_shape=(shape((4, full, tall, levels), f32), tile_sum),
        in_specs=[smem] + [vmem] * 7,
        out_specs=(vmem, vmem),
        scratch_shapes=[
            pltpu.VMEM((4, 2 * HALO, tall, levels), f32),
            pltpu.VMEM((4, 2 * HALO, tall, levels), f32),
        ],
        input_output_aliases={6: 0},
        compiler_params=params,
        cost_estimate=pl.CostEstimate(flops=12_000_000, bytes_accessed=4_000_000, transcendentals=0),
        name="outer",
    )(tile, drag, surface, state, left, right, before, inner_sum)

    message = pl.pallas_call(
        pack_kernel,
        out_shape=shape((tiles, EIGHTH_AT + eighth.shape[0] + REACH * span, levels), f32),
        in_specs=[vmem] * 4,
        out_specs=vmem,
        compiler_params=params,
        name="pack",
    )(sums, outer_sum, state, eighth)
    received = lax.all_to_all(message, "gx", 0, 0, tiled=True)

    out, _ = pl.pallas_call(
        functools.partial(second_kernel, count),
        out_shape=(shape(state.shape, f32), shape(section.shape, f32)),
        in_specs=[smem] + [vmem] * 5,
        out_specs=(whole, vmem),
        scratch_shapes=[
            pltpu.VMEM((precursor.shape[0], span, levels), f32),
            pltpu.VMEM(state.shape, f32),
            pltpu.SemaphoreType.DMA((4,)),
        ],
        input_output_aliases={4: 1},
        compiler_params=params,
        name="second",
    )(tile, drag, surface, state, section, received)
    return out[None]


def solution(mesh):
    in_specs = (P("mem", None, "gx", None, None), P(None, "mem"), P(), P("mem", None), P(), P())
    out_specs = P("mem", None, "gx", None, None)
    return jax.shard_map(local, mesh=mesh, in_specs=in_specs, out_specs=out_specs, check_vma=False)
```
